256 devices in a mesh: section: 16 (over x_lo, y, core), expert: 16 (over z, x_hi).
Axes of the slice: x: 4 (x_hi: 2, x_lo: 2; x = x_hi * 2 + x_lo), y: 4, z: 8, core: 2. Of those that a mesh axis runs over, the one named last changes fastest.
Arguments:
- fwd_acts: bfloat16 [16, 2048, 2048], P('section', 'expert'), may hold values from -6 to 6
- saved_acts: bfloat16 [16, 2048, 2048], P('section', 'expert'), may hold values from -6 to 6
- cotangent: bfloat16 [16, 2048, 2048], P('section', 'expert'), may hold values from -1.5 to 1.5
- gate_w: bfloat16 [16, 16, 2048, 384], P('section', 'expert'), may hold values from -0.125 to 0.125
- up_w: bfloat16 [16, 16, 2048, 384], P('section', 'expert'), may hold values from -0.125 to 0.125
- down_w: bfloat16 [16, 16, 384, 2048], P('section', 'expert'), may hold values from -0.3125 to 0.3125
- routes_f: int32 [16, 2048, 4], P('section', 'expert'), may hold values from 0 to 15, as said below
- slots_f: int32 [16, 2048, 4], P('section', 'expert'), may hold values from 0 to 47, as said below
- gates_f: float32 [16, 2048, 4], P('section', 'expert'), may hold values from 0.2 to 0.6
- routes_b: int32 [16, 2048, 4], P('section', 'expert'), may hold values from 0 to 15, as said below
- slots_b: int32 [16, 2048, 4], P('section', 'expert'), may hold values from 0 to 47, as said below
- gates_b: float32 [16, 2048, 4], P('section', 'expert'), may hold values from 0.2 to 0.6
Outputs:
- fwd_out: bfloat16 [16, 2048, 2048], P('section', 'expert')
- input_grad: bfloat16 [16, 2048, 2048], P('section', 'expert')
- gate_grad: bfloat16 [16, 16, 2048, 384], P('section', 'expert')
- up_grad: bfloat16 [16, 16, 2048, 384], P('section', 'expert')
- down_weight_gradient: bfloat16 [16, 16, 384, 2048], P('section', 'expert')
The draws below stay inside these ranges and needn't reach their ends.
Inputs may be any that keep to these rules, and one draw needn't show every extreme that they name: `routes_f`: each row names 4 different experts, the k-th among experts k * 4 to (k + 1) * 4 - 1. Among the rows of one device no expert is named more than 48 times, and in every such block some expert is named exactly 48 times. `slots_f`: among the rows of one device, the routes that name one expert carry the slot numbers 0 to their count - 1, each once. `routes_b`: as for routes_f. `slots_b`: as for slots_f, with routes_b.
All inputs are finite; a program needn't handle non-finite values.
Results may differ from the reference program's by a relative error of at most 0.0058.
Values may be sent and summed in bfloat16 or wider, within the bound.
No kernel may reach another device: no remote copies, remote signals or barrier semaphores. Data moves between devices by JAX's collectives and lax.ppermute only.
A program may use at most 128 MiB of HBM per device.

```python
import jax
import jax.numpy as jnp
from jax import lax

D = 2048
FF = 384
EXPERTS = 16
TOP = 4
TOK_DEV = 128
TOKENS = 2048
CAP = 40
N_SECTION = 16
N_EXPERT = 16


def route_tables(key, salt):
    key = jax.random.fold_in(key, salt)
    blocks = N_SECTION * TOKENS // TOK_DEV
    group = EXPERTS // TOP
    factor = TOK_DEV // 128
    hot = jax.random.randint(jax.random.fold_in(key, 1), (1, TOP, 1), 0, group)
    spread = jax.random.randint(jax.random.fold_in(key, 2), (blocks, TOP, 2), 0, 17)
    first = 16 + spread[..., 0]
    second = 16 + spread[..., 1]
    counts = jnp.stack([jnp.full_like(first, 48), first, second, 80 - first - second], axis=-1) * factor
    ends = jnp.cumsum(counts, axis=-1)
    starts = ends - counts
    scores = jax.random.randint(jax.random.fold_in(key, 3), (blocks, TOP, 3), 0, 4096) * 4 + jnp.arange(3, dtype=jnp.int32)
    order = jnp.argsort(scores, axis=-1).astype(jnp.int32)
    offsets = jnp.concatenate([jnp.zeros((blocks, TOP, 1), jnp.int32), 1 + order], axis=-1)
    labels = (hot + offsets) % group
    ranks = jax.random.randint(jax.random.fold_in(key, 4), (blocks, TOP, TOK_DEV), 0, 2 ** 20) * TOK_DEV + jnp.arange(TOK_DEV, dtype=jnp.int32)
    position = jnp.argsort(ranks, axis=-1).astype(jnp.int32)
    bucket = jnp.zeros_like(position)
    for level in range(3):
        bucket = bucket + (position >= ends[..., level:level + 1]).astype(jnp.int32)
    slots = position - jnp.take_along_axis(starts, bucket, axis=-1)
    column = jnp.arange(TOP, dtype=jnp.int32)[None, :, None]
    experts = column * group + jnp.take_along_axis(labels, bucket, axis=-1)
    experts = jnp.transpose(experts, (0, 2, 1)).reshape(N_SECTION, TOKENS, TOP)
    slots = jnp.transpose(slots, (0, 2, 1)).reshape(N_SECTION, TOKENS, TOP)
    return (experts.astype(jnp.int32), slots.astype(jnp.int32))


def draw_routes_f(key, part):
    tables = route_tables(key, 11)
    return tables[0]


def draw_slots_f(key, part):
    tables = route_tables(key, 11)
    return tables[1]


def draw_routes_b(key, part):
    tables = route_tables(key, 23)
    return tables[0]


def draw_slots_b(key, part):
    tables = route_tables(key, 23)
    return tables[1]


def levels(own_key, shape, shards, smallest, high):
    factor_of, own = 1.0, jax.random.fold_in(own_key, 6)
    for axis_at, blocks in shards:
        heights = jnp.exp(jax.random.uniform(jax.random.fold_in(own, axis_at), (blocks,), jnp.float32, smallest / len(shards), high / len(shards)))
        factor_of = factor_of * jnp.repeat(heights, shape[axis_at] // blocks).reshape([-1 if axis == axis_at else 1 for axis in range(len(shape))])
    return factor_of


def normal_values(own_key, extent, scale, bound, split=(), held_as=jnp.bfloat16):
    values = scale * jax.random.normal(own_key, extent, jnp.float32)
    if split:
        values = values * levels(own_key, extent, split, -0.22, 0.18)
    return jnp.clip(values, -bound, bound).astype(held_as)


def setup_inputs(seed: int = 0) -> dict:
    streams_of = jax.random.split(jax.random.key(seed), 13)
    fwd_acts = normal_values(streams_of[0], (N_SECTION, TOKENS, D), 1.0, 6.0, ((0, 16), (1, 16)))
    saved_acts = normal_values(streams_of[1], (N_SECTION, TOKENS, D), 1.0, 6.0, ((0, 16), (1, 16)))
    cotangent = normal_values(streams_of[2], (N_SECTION, TOKENS, D), 0.25, 1.5, ((0, 16), (1, 16)))
    gate_w = normal_values(streams_of[3], (N_SECTION, EXPERTS, D, FF), D ** -0.5, 0.125, ((0, 16), (1, 16)))
    up_w = normal_values(streams_of[4], (N_SECTION, EXPERTS, D, FF), D ** -0.5, 0.125, ((0, 16), (1, 16)))
    down_w = normal_values(streams_of[5], (N_SECTION, EXPERTS, FF, D), FF ** -0.5, 0.3125, ((0, 16), (1, 16)))
    routes_f = draw_routes_f(jax.random.fold_in(streams_of[12], 71), 0)
    slots_f = draw_slots_f(jax.random.fold_in(streams_of[12], 71), 0)
    gates_f = jnp.clip(0.2 + 0.400000021 * jax.random.uniform(streams_of[8], (N_SECTION, TOKENS, TOP), jnp.float32) ** levels(streams_of[8], (N_SECTION, TOKENS, TOP), ((0, 16), (1, 16)), -0.2, 0.2), 0.2, 0.6)
    routes_b = draw_routes_b(jax.random.fold_in(streams_of[12], 71), 0)
    slots_b = draw_slots_b(jax.random.fold_in(streams_of[12], 71), 0)
    gates_b = jnp.clip(0.2 + 0.400000021 * jax.random.uniform(streams_of[11], (N_SECTION, TOKENS, TOP), jnp.float32) ** levels(streams_of[11], (N_SECTION, TOKENS, TOP), ((0, 16), (1, 16)), -0.2, 0.2), 0.2, 0.6)
    return {"fwd_acts": fwd_acts, "saved_acts": saved_acts, "cotangent": cotangent, "gate_w": gate_w, "up_w": up_w, "down_w": down_w, "routes_f": routes_f, "slots_f": slots_f, "gates_f": gates_f, "routes_b": routes_b, "slots_b": slots_b, "gates_b": gates_b}


def slot_index(routes, slots):
    source = (jnp.arange(TOKENS, dtype=jnp.int32) // TOK_DEV)[:, None]
    kept = slots < CAP
    place = routes * (N_EXPERT * CAP) + source * CAP + slots
    dump = EXPERTS * N_EXPERT * CAP
    return jnp.where(kept, place, dump).astype(jnp.int32), kept


def scatter_into_buffer(rows, place):
    total = EXPERTS * N_EXPERT * CAP
    buffer = jnp.zeros((total + 1, D), rows.dtype)
    buffer = buffer.at[place.reshape(-1)].set(rows.reshape(-1, D))
    return buffer[:total].reshape(EXPERTS, N_EXPERT * CAP, D)


def pick_rows(buffer, place):
    flat = jnp.concatenate([buffer.reshape(-1, D), jnp.zeros((1, D), buffer.dtype)], axis=0)
    return flat[place].astype(jnp.float32)


def one_section(inputs):
    layer_in, back_x, grad_out, wg, wu, wd, rf, sf, gf, rb, sb, gb = inputs
    wg32 = wg.astype(jnp.float32)
    wu32 = wu.astype(jnp.float32)
    down_weight_float32 = wd.astype(jnp.float32)
    place_f, kept_f = slot_index(rf, sf)
    xbuf = scatter_into_buffer(jnp.broadcast_to(layer_in[:, None, :], (TOKENS, TOP, D)), place_f).astype(jnp.float32)
    act_a = jnp.einsum("erd,edf->erf", xbuf, wg32)
    act_b = jnp.einsum("erd,edf->erf", xbuf, wu32)
    hidden = (act_a * jax.nn.sigmoid(act_a) * act_b).astype(jnp.bfloat16)
    out_rows = jnp.einsum("erf,efd->erd", hidden.astype(jnp.float32), down_weight_float32).astype(jnp.bfloat16)
    weights = jnp.where(kept_f, gf, jnp.float32(0.0))
    picked = pick_rows(out_rows, place_f)
    fwd_out = (layer_in.astype(jnp.float32) + jnp.sum(picked * weights[..., None], axis=1)).astype(jnp.bfloat16)

    placement_backward, kept_b = slot_index(rb, sb)
    gradient_rows = (gb[..., None] * grad_out[:, None, :].astype(jnp.float32)).astype(jnp.bfloat16)
    xbuf_b = scatter_into_buffer(jnp.broadcast_to(back_x[:, None, :], (TOKENS, TOP, D)), placement_backward).astype(jnp.float32)
    gradient_buffer_backward = scatter_into_buffer(gradient_rows, placement_backward).astype(jnp.float32)
    act_a = jnp.einsum("erd,edf->erf", xbuf_b, wg32)
    act_b = jnp.einsum("erd,edf->erf", xbuf_b, wu32)
    sig = jax.nn.sigmoid(act_a)
    silu_a = act_a * sig
    hidden_backward = (silu_a * act_b).astype(jnp.bfloat16)
    hidden_gradient = jnp.einsum("qto,qyo->qty", gradient_buffer_backward, down_weight_float32)
    d_a = (hidden_gradient * act_b * sig * (1.0 + act_a * (1.0 - sig))).astype(jnp.bfloat16).astype(jnp.float32)
    d_b = (hidden_gradient * silu_a).astype(jnp.bfloat16).astype(jnp.float32)
    dx_rows = (jnp.einsum("erf,edf->erd", d_a, wg32) + jnp.einsum("erf,edf->erd", d_b, wu32)).astype(jnp.bfloat16)
    gate_grad = jnp.einsum("erd,erf->edf", xbuf_b, d_a).astype(jnp.bfloat16)
    up_grad = jnp.einsum("erd,erf->edf", xbuf_b, d_b).astype(jnp.bfloat16)
    down_weight_gradient = jnp.einsum("cvm,cvk->cmk", hidden_backward.astype(jnp.float32), gradient_buffer_backward).astype(jnp.bfloat16)
    keep_b = jnp.where(kept_b, jnp.float32(1.0), jnp.float32(0.0))
    picked_b = pick_rows(dx_rows, placement_backward)
    input_grad = (grad_out.astype(jnp.float32) + jnp.sum(picked_b * keep_b[..., None], axis=1)).astype(jnp.bfloat16)
    return fwd_out, input_grad, gate_grad, up_grad, down_weight_gradient


def reference(fwd_acts, saved_acts, cotangent, gate_w, up_w, down_w, routes_f, slots_f, gates_f, routes_b, slots_b, gates_b):
    layer_in = jnp.roll(fwd_acts, 1, axis=0)
    grad_out = jnp.roll(cotangent, -1, axis=0)
    results = lax.map(one_section, (layer_in, saved_acts, grad_out, gate_w, up_w, down_w, routes_f, slots_f, gates_f, routes_b, slots_b, gates_b))
    return (results[0], results[1], results[2], results[3], results[4])
```

```python
import functools

import jax
import jax.numpy as jnp
from jax import lax
from jax.experimental import pallas as pl
from jax.experimental.pallas import tpu as pltpu
from jax.sharding import PartitionSpec as P

CAP = 40
NZ = 8
CODE = 64
F32 = jnp.float32
BF16 = jnp.bfloat16
AXES = ("section", "expert")
VMEM = pl.BlockSpec(memory_space=pltpu.VMEM)
SMEM = pl.BlockSpec(memory_space=pltpu.SMEM)

BLOCKS = (
    (-1, 0), (1, 0), (-1, 1), (1, 1),
    (-2, 0), (2, 0), (-2, 1), (2, 1),
    (0, 0), (-3, 0), (0, 1), (-3, 1),
    (-4, 0), (-4, 1), (3, 0), (3, 1),
)


def hop(block, dz, flip):
    sections, experts = lax.axis_size("section"), lax.axis_size("expert")
    pairs = []
    for section in range(sections):
        sign = 1 - 2 * (section % 2)
        for expert in range(experts):
            z, line = divmod(expert, 2)
            to = ((z + sign * dz) % NZ) * 2 + (line ^ flip)
            pairs.append((section * experts + expert, section * experts + to))
    return lax.ppermute(block, AXES, pairs)


def node(where, dz):
    return (where[0] + dz * where[2]) & (NZ - 1)


def onehot(meta, where, table, source, at, flip):
    z = node(where, at)
    line = where[1]
    expert = z * 2 + (1 - line if flip else line)
    src = node(where, source[0]) * 2 + (1 - line if source[1] else line)
    code = meta[src, pl.ds(table + lax.shift_right_logical(z, 1), 1), :]
    slot = lax.broadcasted_iota(jnp.int32, (CAP, code.shape[-1]), 0) + expert * CODE
    return code == slot.astype(F32)


def gate_of(meta, where, table, source, at, mask):
    line = where[1]
    src = node(where, source[0]) * 2 + (1 - line if source[1] else line)
    gate = meta[src, pl.ds(table + 4 + lax.shift_right_logical(node(where, at), 1), 1), :]
    return jnp.sum(jnp.where(mask, gate, 0.0), axis=1, keepdims=True)


def pick(meta, where, table, block, source, places, gated):
    masks = [onehot(meta, where, table, source, at, flip) for at, flip in places]
    chosen = jnp.concatenate([m.astype(F32) for m in masks], axis=0).astype(BF16)
    rows = jnp.dot(chosen, block, preferred_element_type=F32)
    parts = [rows[i * CAP : (i + 1) * CAP] for i in range(len(places))]
    if gated:
        parts = [
            part * gate_of(meta, where, table, source, at, mask)
            for part, mask, (at, _) in zip(parts, masks, places)
        ]
    return parts


def two(a, b):
    return jnp.concatenate([a, b], axis=0).astype(BF16)


HERE = ((0, 0), (0, 1))


def take_kernel(table, gated, sources, ahead, where, meta, a_ref, b_ref, own_ref, oth_ref, *far):
    places = [HERE, HERE]
    if ahead is not None:
        places[ahead[0]] = HERE + ((ahead[1], 0), (ahead[1], 1))
    got = [
        pick(meta, where, table, ref[...], source, place, gated)
        for ref, source, place in zip((a_ref, b_ref), sources, places)
    ]
    own_ref[...] = two(got[0][0], got[1][0])
    oth_ref[...] = two(got[0][1], got[1][1])
    if ahead is not None:
        far[0][...] = got[ahead[0]][2].astype(BF16)
        far[1][...] = got[ahead[0]][3].astype(BF16)


def call(kernel, outs, args, flops, limit, name, scratch=()):
    size = sum(a.size * a.dtype.itemsize for a in args) + sum(
        o.size * jnp.dtype(o.dtype).itemsize for o in outs
    )
    return pl.pallas_call(
        kernel,
        out_shape=outs,
        in_specs=[SMEM] + [VMEM] * (len(args) - 1),
        out_specs=[VMEM] * len(outs),
        scratch_shapes=scratch,
        compiler_params=pltpu.CompilerParams(vmem_limit_bytes=limit << 20),
        cost_estimate=pl.CostEstimate(flops=flops, bytes_accessed=size, transcendentals=0),
        name=name,
    )(*args)


def shape(rows, width, dtype=BF16):
    return jax.ShapeDtypeStruct((rows, width), dtype)


def take(where, meta, a, b, sources, ahead, table, gated, name):
    width = a.shape[-1]
    outs = [shape(2 * CAP, width)] * 2 + ([shape(CAP, width)] * 2 if ahead is not None else [])
    return call(
        functools.partial(take_kernel, table, gated, sources, ahead),
        outs,
        (where, meta, a, b),
        2 * 240 * 128 * width,
        24,
        name,
    )


def dispatch(where, meta, block, table, gated, name):
    r1, l1 = hop(block, 1, 0), hop(block, -1, 0)
    r2, l2 = hop(r1, 1, 0), hop(l1, -1, 0)
    r3 = hop(r2, 1, 0)
    u1, v1 = take(where, meta, r1, l1, ((-1, 0), (1, 0)), None, table, gated, name + "_near")
    x1 = hop(v1, 0, 1)
    u2, v2, e_s, e_d = take(where, meta, r2, l2, ((-2, 0), (2, 0)), (1, -1), table, gated, name + "_mid")
    l3s, l3d = hop(e_s, -1, 0), hop(e_d, -1, 1)
    x2 = hop(v2, 0, 1)
    u3, v3, e_s, e_d = take(where, meta, block, r3, ((0, 0), (-3, 0)), (1, 1), table, gated, name + "_far")
    r4s, r4d = hop(e_s, 1, 0), hop(e_d, 1, 1)
    x3 = hop(v3, 0, 1)
    return (u1, x1, u2, x2, u3, x3, r4s, r4d, l3s, l3d), r3


def assemble(units, x_ref):
    for i in range(6):
        x_ref[i * 80 : (i + 1) * 80, :] = units[i][...]
    x_ref[480:560, :] = two(units[6][...].astype(F32), units[7][...].astype(F32))
    x_ref[560:640, :] = two(units[8][...].astype(F32), units[9][...].astype(F32))


def spread_out(value_of, outs):
    for i in range(6):
        outs[i][...] = value_of(i).astype(BF16)
    for i, (s, d) in ((6, (6, 7)), (7, (8, 9))):
        rows = value_of(i)
        outs[s][...] = rows[:CAP].astype(BF16)
        outs[d][...] = rows[CAP:].astype(BF16)


TILE = 320


def forward_kernel(table, where, meta, *refs):
    units, (gate_w, up_w, down_w), outs, (x_ref, o_ref) = refs[:10], refs[10:13], refs[13:23], refs[23:]
    assemble(units, x_ref)

    @pl.loop(0, 640 // TILE)
    def _(i):
        rows = pl.ds(pl.multiple_of(i * TILE, TILE), TILE)
        x = x_ref[rows, :]
        a = jnp.dot(x, gate_w[...], preferred_element_type=F32)
        b = jnp.dot(x, up_w[...], preferred_element_type=F32)
        h = (a * jax.nn.sigmoid(a) * b).astype(BF16)
        o_ref[rows, :] = jnp.dot(h, down_w[...], preferred_element_type=F32)

    def gated(i):
        gates = []
        for source in BLOCKS[2 * i : 2 * i + 2]:
            mask = onehot(meta, where, table, source, 0, 0)
            gates.append(gate_of(meta, where, table, source, 0, mask))
        return o_ref[i * 80 : (i + 1) * 80, :] * jnp.concatenate(gates, axis=0)

    spread_out(gated, outs)


def recompute_kernel(where, *refs):
    units, (gate_w, up_w), (x_ref, h_ref, p_ref, q_ref) = refs[:10], refs[10:12], refs[12:]
    assemble(units, x_ref)

    @pl.loop(0, 640 // TILE)
    def _(i):
        rows = pl.ds(pl.multiple_of(i * TILE, TILE), TILE)
        x = x_ref[rows, :]
        a = jnp.dot(x, gate_w[...], preferred_element_type=F32)
        b = jnp.dot(x, up_w[...], preferred_element_type=F32)
        sig = jax.nn.sigmoid(a)
        silu = a * sig
        h_ref[rows, :] = (silu * b).astype(BF16)
        p_ref[rows, :] = b * sig * (1.0 + a * (1.0 - sig))
        q_ref[rows, :] = silu


NT = (((1,), (1,)), ((), ()))


def backward_kernel(where, *refs):
    units, (p_ref, q_ref, gate_w, up_w, down_w) = refs[:10], refs[10:15]
    outs, (g_ref, da_ref, db_ref), (o_ref,) = refs[15:25], refs[25:28], refs[28:]
    assemble(units, g_ref)

    @pl.loop(0, 640 // TILE)
    def _(i):
        rows = pl.ds(pl.multiple_of(i * TILE, TILE), TILE)
        dh = lax.dot_general(g_ref[rows, :], down_w[...], NT, preferred_element_type=F32)
        da = (dh * p_ref[rows, :]).astype(BF16)
        db = (dh * q_ref[rows, :]).astype(BF16)
        da_ref[rows, :] = da
        db_ref[rows, :] = db
        o_ref[rows, :] = lax.dot_general(da, gate_w[...], NT, preferred_element_type=F32) + lax.dot_general(
            db, up_w[...], NT, preferred_element_type=F32
        )

    spread_out(lambda i: o_ref[i * 80 : (i + 1) * 80, :], outs)


TN = (((0,), (0,)), ((), ()))


def expand(meta, where, table, dest, half, own, other):
    total = 0.0
    for flip, ref in ((0, own), (1, other)):
        mask = onehot(meta, where, table, (dest, 0), 0, flip).astype(F32)
        empty = jnp.zeros_like(mask)
        mask = two(mask, empty) if half == 0 else two(empty, mask)
        total = total + lax.dot_general(mask, ref[...], TN, preferred_element_type=F32)
    return total


def begin_kernel(table, dest, half, at, where, meta, own, other, far_s, far_d, out):
    total = expand(meta, where, table, dest, half, own, other)
    for flip, ref in ((0, far_s), (1, far_d)):
        mask = onehot(meta, where, table, (dest, 0), at, flip).astype(F32).astype(BF16)
        total = total + lax.dot_general(mask, ref[...], TN, preferred_element_type=F32)
    out[...] = total.astype(BF16)


def onward_kernel(table, dest, half, where, meta, own, other, *refs):
    total = expand(meta, where, table, dest, half, own, other)
    for ref in refs[:-1]:
        total = total + ref[...].astype(F32)
    refs[-1][...] = total.astype(BF16)


def begin(where, meta, table, dest, half, at, own, other, far_s, far_d, name):
    width = own.shape[-1]
    return call(
        functools.partial(begin_kernel, table, dest, half, at),
        [shape(128, width)],
        (where, meta, own, other, far_s, far_d),
        2 * 240 * 128 * width,
        16,
        name,
    )[0]


def onward(where, meta, table, dest, half, own, other, dense, name):
    width = own.shape[-1]
    return call(
        functools.partial(onward_kernel, table, dest, half),
        [shape(128, width)],
        (where, meta, own, other, *dense),
        2 * 160 * 128 * width,
        16,
        name,
    )[0]


def combine(where, meta, rows, base, table, name):
    u1, v1, u2, v2, u3, v3, r4s, r4d, l3s, l3d = rows
    r4s, r4d = hop(r4s, -1, 0), hop(r4d, -1, 1)
    l3s, l3d = hop(l3s, 1, 0), hop(l3d, 1, 1)
    x3, x2, x1 = hop(v3, 0, 1), hop(v2, 0, 1), hop(v1, 0, 1)
    right = hop(begin(where, meta, table, -3, 1, 1, u3, x3, r4s, r4d, name + "_r3"), -1, 0)
    left = hop(begin(where, meta, table, 2, 1, -1, u2, x2, l3s, l3d, name + "_l2"), 1, 0)
    right = hop(onward(where, meta, table, -2, 0, u2, x2, (right,), name + "_r2"), -1, 0)
    left = hop(onward(where, meta, table, 1, 1, u1, x1, (left,), name + "_l1"), 1, 0)
    right = hop(onward(where, meta, table, -1, 0, u1, x1, (right,), name + "_r1"), -1, 0)
    return onward(where, meta, table, 0, 0, u3, x3, (right, left, base), name + "_end")


def along_sections(block, distance):
    count = lax.axis_size("section")
    return lax.ppermute(block, "section", [((i - distance) % count, i) for i in range(count)])


def tables(routes_f, slots_f, gates_f, routes_b, slots_b, gates_b):
    code_f = (routes_f * CODE + slots_f).astype(F32)
    code_b = (routes_b * CODE + slots_b).astype(F32)
    return jnp.concatenate([code_f, gates_f, code_b, gates_b], axis=-1).T


def local(
    fwd_acts, saved_acts, cotangent, gate_w, up_w, down_w, routes_f, slots_f, gates_f, routes_b, slots_b, gates_b
):
    gate_w, up_w, down_w = gate_w[0, 0], up_w[0, 0], down_w[0, 0]
    back_x = saved_acts[0]
    grad_out = along_sections(cotangent, -1)[0]
    layer_in = along_sections(fwd_acts, 1)[0]
    meta = lax.all_gather(
        tables(routes_f[0], slots_f[0], gates_f[0], routes_b[0], slots_b[0], gates_b[0]), "expert"
    )
    at = lax.axis_index("expert")
    sign = 1 - 2 * (lax.axis_index("section") % 2)
    where = jnp.stack([at // 2, at % 2, sign]).astype(jnp.int32)
    width, hidden = gate_w.shape
    products = 2 * 640 * width * hidden

    x_units, _ = dispatch(where, meta, back_x, 8, False, "x")
    g_units, mark = dispatch(where, meta, grad_out, 8, True, "g")
    xb, hb, p, q = call(
        recompute_kernel,
        [shape(640, width), shape(640, hidden), shape(640, hidden, F32), shape(640, hidden, F32)],
        (where, *x_units, gate_w, up_w),
        2 * products,
        32,
        "recompute",
    )
    layer_late, _ = lax.optimization_barrier((layer_in, mark))
    f_units, _ = dispatch(where, meta, layer_late, 0, False, "f")
    ten = [shape(80, width)] * 6 + [shape(CAP, width)] * 4
    *dx_rows, gb, da, db = call(
        backward_kernel,
        ten + [shape(640, width), shape(640, hidden), shape(640, hidden)],
        (where, *g_units, p, q, gate_w, up_w, down_w),
        3 * products,
        40,
        "backward",
        [pltpu.VMEM((640, width), F32)],
    )
    input_grad = combine(where, meta, dx_rows, grad_out, 8, "dx")
    out_rows = call(
        functools.partial(forward_kernel, 0),
        ten,
        (where, meta, *f_units, gate_w, up_w, down_w),
        3 * products,
        40,
        "forward",
        [pltpu.VMEM((640, width), BF16), pltpu.VMEM((640, width), F32)],
    )
    fwd_out = combine(where, meta, out_rows, layer_in, 0, "y")
    gate_grad = lax.dot_general(xb, da, TN, preferred_element_type=F32).astype(BF16)
    up_grad = lax.dot_general(xb, db, TN, preferred_element_type=F32).astype(BF16)
    down_grad = lax.dot_general(hb, gb, TN, preferred_element_type=F32).astype(BF16)
    return fwd_out[None], input_grad[None], gate_grad[None, None], up_grad[None, None], down_grad[None, None]


def solution(mesh):
    tokens = P("section", "expert", None)
    weights = P("section", "expert", None, None)
    return jax.shard_map(
        local,
        mesh=mesh,
        in_specs=(tokens,) * 3 + (weights,) * 3 + (tokens,) * 6,
        out_specs=(tokens,) * 2 + (weights,) * 3,
        check_vma=False,
    )
```

```python
import functools

import jax
import jax.numpy as jnp
from jax import lax
from jax.experimental import pallas as pl
from jax.experimental.pallas import tpu as pltpu
from jax.sharding import PartitionSpec as P

CAP = 40
NZ = 8
CODE = 64
F32 = jnp.float32
BF16 = jnp.bfloat16
AXES = ("section", "expert")
VMEM = pl.BlockSpec(memory_space=pltpu.VMEM)
SMEM = pl.BlockSpec(memory_space=pltpu.SMEM)


def hop(block, dz, flip, from_section=0):
    sections, experts = lax.axis_size("section"), lax.axis_size("expert")
    pairs = []
    for section in range(sections):
        sign = 1 - 2 * (section % 2)
        sender = (section + from_section) % sections
        for expert in range(experts):
            z, line = divmod(expert, 2)
            to = ((z + sign * dz) % NZ) * 2 + (line ^ flip)
            pairs.append((sender * experts + expert, section * experts + to))
    return lax.ppermute(block, AXES, pairs)


def after(value, *earlier):
    return lax.optimization_barrier((value, *earlier))[0]


def call(kernel, outs, args, flops, limit, name, scratch=()):
    size = sum(a.size * a.dtype.itemsize for a in args) + sum(
        o.size * jnp.dtype(o.dtype).itemsize for o in outs
    )
    return pl.pallas_call(
        kernel,
        out_shape=outs,
        in_specs=[SMEM] + [VMEM] * (len(args) - 1),
        out_specs=[VMEM] * len(outs),
        scratch_shapes=scratch,
        compiler_params=pltpu.CompilerParams(vmem_limit_bytes=limit << 20),
        cost_estimate=pl.CostEstimate(flops=flops, bytes_accessed=size, transcendentals=0),
        name=name,
    )(*args)


def shape(rows, width, dtype=BF16):
    return jax.ShapeDtypeStruct((rows, width), dtype)


def columns(routes_f, slots_f, gates_f, routes_b, slots_b, gates_b):
    gates = jnp.concatenate([gates_f, gates_b], axis=-1)
    high = lax.reduce_precision(gates, 8, 7)
    mid = lax.reduce_precision(gates - high, 8, 7)
    ints = [part.astype(F32) for part in (routes_f, routes_b, slots_f, slots_b)]
    every = jnp.concatenate([*ints, high, mid, gates - high - mid], axis=-1)
    return jnp.pad(every, ((0, 0), (0, 128 - every.shape[-1]))).astype(BF16)


def table_of(block, width):
    flat = block[:, width : width + 128].astype(F32).T
    codes = flat[0:8] * CODE + flat[8:16]
    return jnp.concatenate([codes, flat[16:24] + flat[24:32] + flat[32:40]], axis=0)


def group(where, at):
    return lax.shift_right_logical((where[0] + at * where[2]) & (NZ - 1), 1)


def onehot(where, table, first, at, flip):
    z = (where[0] + at * where[2]) & (NZ - 1)
    expert = z * 2 + (1 - where[1] if flip else where[1])
    code = table[pl.ds(first + group(where, at), 1), :]
    slot = lax.broadcasted_iota(jnp.int32, (CAP, code.shape[-1]), 0) + expert * CODE
    return (code == slot.astype(F32)).astype(F32)


def gate_row(where, table, first, at):
    return table[pl.ds(8 + first + group(where, at), 1), :]


def stack(*parts):
    return jnp.concatenate(parts, axis=0).astype(BF16)


def pick(where, table, first, block, places, gated):
    chosen = [onehot(where, table, first, at, flip) for at, flip in places]
    rows = jnp.dot(stack(*chosen), block, preferred_element_type=F32)
    if gated:
        gates = [
            jnp.sum(mask * gate_row(where, table, first, at), axis=1, keepdims=True)
            for mask, (at, _) in zip(chosen, places)
        ]
        rows = rows * jnp.concatenate(gates, axis=0)
    return [rows[i * CAP : (i + 1) * CAP] for i in range(len(places))]


HERE = ((0, 0), (0, 1))


def near_kernel(first, width, where, near, r1, l1, table0, table_r, table_l, own, other):
    got = [
        pick(where, table, first, block[...], HERE, False)
        for block, table in ((near, table0), (r1, table_r), (l1, table_l))
    ]
    own[...] = stack(*[g[0] for g in got])
    other[...] = stack(*[g[1] for g in got])


def mid_kernel(first, width, where, r2, l2, table_r, table_l, own, other, end):
    a = pick(where, table_r, first, r2[...], HERE, False)
    b = pick(where, table_l, first, l2[...], HERE + ((-1, 0), (-1, 1)), False)
    own[...] = stack(a[0], b[0])
    other[...] = stack(a[1], b[1])
    end[...] = stack(b[2], b[3])


def far_kernel(first, width, where, r3, l3, table3, own, other, same, cross):
    got = pick(where, table3, first, r3[...], HERE + ((1, 0), (1, 1)), False)
    own[...] = got[0].astype(BF16)
    other[...] = stack(got[1], l3[...].astype(F32)[CAP:])
    same[...] = got[2].astype(BF16)
    cross[...] = got[3].astype(BF16)


TABLE = (16, 128)


def halves(width):
    return (
        (False, slice(0, width), slice(0, width)),
        (True, slice(width + 128, 2 * width + 128), slice(width, 2 * width)),
    )


def both_near_kernel(width, where, near_x, near_g, r1, l1, own, other, *tables):
    for block, table in zip((near_x, r1, l1), tables):
        table[...] = table_of(block, width)
    for gated, of, cols in halves(width):
        near = near_g[...] if gated else near_x[:, cols]
        got = [
            pick(where, table, 4, block, HERE, gated)
            for block, table in zip((near, r1[:, of], l1[:, of]), tables)
        ]
        own[:, cols] = stack(*[g[0] for g in got])
        other[:, cols] = stack(*[g[1] for g in got])


def both_mid_kernel(width, where, r2, l2, own, other, end, table_r, table_l):
    table_r[...] = table_of(r2, width)
    table_l[...] = table_of(l2, width)
    for gated, of, cols in halves(width):
        a = pick(where, table_r, 4, r2[:, of], HERE, gated)
        b = pick(where, table_l, 4, l2[:, of], HERE + ((-1, 0), (-1, 1)), gated)
        own[:, cols] = stack(a[0], b[0])
        other[:, cols] = stack(a[1], b[1])
        end[:, cols] = stack(b[2], b[3])


def both_far_kernel(width, where, r3, l3, own, other, same, cross, table):
    table[...] = table_of(r3, width)
    for gated, of, cols in halves(width):
        got = pick(where, table, 4, r3[:, of], HERE + ((1, 0), (1, 1)), gated)
        own[:, cols] = got[0].astype(BF16)
        other[:, cols] = stack(got[1], l3[:, cols].astype(F32)[CAP:])
        same[:, cols] = got[2].astype(BF16)
        cross[:, cols] = got[3].astype(BF16)


def single(kernel, where, blocks, rows, width, name):
    return call(
        functools.partial(kernel, 0, width),
        [shape(r, width) for r in rows],
        (where, *blocks),
        2 * 240 * 128 * width,
        24,
        name,
    )


def both(kernel, where, blocks, rows, tables, width, name):
    outs = [shape(r, 2 * width) for r in rows] + [shape(*TABLE, F32)] * tables
    return call(functools.partial(kernel, width), outs, (where, *blocks), 4 * 240 * 128 * width, 32, name)


def assemble(near, far_units, x_ref, cols=slice(None)):
    x_ref[0:400, :] = stack(*[unit[:, cols].astype(F32) for unit in near])
    u3, l3, x3, r4s, r4d = far_units
    x_ref[400:480, :] = stack(u3[:, cols].astype(F32), l3[:, cols].astype(F32)[:CAP])
    x_ref[480:560, :] = x3[:, cols]
    x_ref[560:640, :] = stack(r4s[:, cols].astype(F32), r4d[:, cols].astype(F32))


PARTS = ((0, 200), (200, 400), (400, 440), (440, 480), (480, 560), (560, 600), (600, 640))


def part(o_ref, outs):
    for out, (first, last) in zip(outs, PARTS):
        out[...] = o_ref[first:last, :].astype(BF16)


def parts(width):
    return [shape(last - first, width) for first, last in PARTS]


TILE = 640
NT = (((1,), (1,)), ((), ()))
TN = (((0,), (0,)), ((), ()))


def tiles(body):
    @pl.loop(0, 640 // TILE)
    def _(i):
        body(pl.ds(pl.multiple_of(i * TILE, TILE), TILE))


def forward_kernel(where, *refs):
    units, (gate_w, up_w, down_w), outs, (x_ref, o_ref) = refs[:9], refs[9:12], refs[12:19], refs[19:]
    assemble(units[:4], units[4:], x_ref)

    @tiles
    def _(rows):
        x = x_ref[rows, :]
        a = jnp.dot(x, gate_w[...], preferred_element_type=F32)
        b = jnp.dot(x, up_w[...], preferred_element_type=F32)
        h = (a * jax.nn.sigmoid(a) * b).astype(BF16)
        o_ref[rows, :] = jnp.dot(h, down_w[...], preferred_element_type=F32)

    part(o_ref, outs)


def backward_kernel(width, where, *refs):
    units, (gate_w, up_w, down_w) = refs[:9], refs[9:12]
    outs, (x_ref, g_ref, h_ref, da_ref, db_ref), (o_ref,) = refs[12:19], refs[19:24], refs[24:]
    assemble(units[:4], units[4:], x_ref, slice(0, width))
    assemble(units[:4], units[4:], g_ref, slice(width, 2 * width))

    @tiles
    def _(rows):
        x = x_ref[rows, :]
        a = jnp.dot(x, gate_w[...], preferred_element_type=F32)
        b = jnp.dot(x, up_w[...], preferred_element_type=F32)
        sig = jax.nn.sigmoid(a)
        silu = a * sig
        h_ref[rows, :] = (silu * b).astype(BF16)
        dh = lax.dot_general(g_ref[rows, :], down_w[...], NT, preferred_element_type=F32)
        da = (dh * b * sig * (1.0 + a * (1.0 - sig))).astype(BF16)
        db = (dh * silu).astype(BF16)
        da_ref[rows, :] = da
        db_ref[rows, :] = db
        o_ref[rows, :] = lax.dot_general(da, gate_w[...], NT, preferred_element_type=F32) + lax.dot_general(
            db, up_w[...], NT, preferred_element_type=F32
        )

    part(o_ref, outs)


def placed(rows, masks):
    out, at = [], 0
    for start, mask in masks:
        if start > at:
            out.append(jnp.zeros((start - at, mask.shape[1]), F32))
        out.append(mask)
        at = start + CAP
    if at < rows:
        out.append(jnp.zeros((rows - at, masks[0][1].shape[1]), F32))
    return stack(*out)


def product(mask, rows):
    return lax.dot_general(mask, rows, TN, preferred_element_type=F32)


def weigh(where, table, first, at, gated, rows):
    if not gated:
        return rows
    row = gate_row(where, table, first, at)
    count = row.shape[-1]
    same = lax.broadcasted_iota(jnp.int32, (count, count), 0) == lax.broadcasted_iota(jnp.int32, (count, count), 1)
    return rows * jnp.sum(jnp.where(same, row, 0.0), axis=1, keepdims=True)


def local_sum(where, table, first, gated, own, other, start):
    total = 0.0
    for flip, ref in ((0, own), (1, other)):
        mask = placed(ref.shape[0], [(start, onehot(where, table, first, 0, flip))])
        total = total + product(mask, ref[...])
    return weigh(where, table, first, 0, gated, total)


def sum3_kernel(first, gated, where, y3, x3, r4s, r4d, l3, table, right, left):
    total = local_sum(where, table, first, gated, y3, x3, 0)
    ahead = 0.0
    for flip, ref in ((0, r4s), (1, r4d)):
        ahead = ahead + product(onehot(where, table, first, 1, flip).astype(BF16), ref[...])
    right[...] = (total + weigh(where, table, first, 1, gated, ahead)).astype(BF16)
    left[...] = stack(l3[...].astype(F32), x3[...].astype(F32)[CAP:])


def sum2_kernel(first, gated, where, y12, x12, got_r, got_l, table_r, table_l, right, left):
    right[...] = (got_r[...].astype(F32) + local_sum(where, table_r, first, gated, y12, x12, 120)).astype(BF16)
    masks = [(0, onehot(where, table_l, first, -1, 0)), (CAP, onehot(where, table_l, first, -1, 1))]
    ahead = weigh(where, table_l, first, -1, gated, product(placed(80, masks), got_l[...]))
    left[...] = (ahead + local_sum(where, table_l, first, gated, y12, x12, 160)).astype(BF16)


def sum1_kernel(first, gated, where, y12, x12, got_r, got_l, table_r, table_l, right, left):
    right[...] = (got_r[...].astype(F32) + local_sum(where, table_r, first, gated, y12, x12, 40)).astype(BF16)
    left[...] = (got_l[...].astype(F32) + local_sum(where, table_l, first, gated, y12, x12, 80)).astype(BF16)


def sum0_kernel(first, gated, where, y12, x12, got_r, got_l, base, table, out):
    total = local_sum(where, table, first, gated, y12, x12, 0)
    total = total + got_r[...].astype(F32) + got_l[...].astype(F32)
    out[...] = (base[...].astype(F32) + total).astype(BF16)


def summed(kernel, where, args, first, gated, rows, name):
    width = args[0].shape[-1]
    return call(
        functools.partial(kernel, first, gated),
        [shape(r, width) for r in rows],
        (where, *args),
        2 * 320 * 128 * width,
        24,
        name,
    )


def local(
    fwd_acts, saved_acts, cotangent, gate_w, up_w, down_w, routes_f, slots_f, gates_f, routes_b, slots_b, gates_b
):
    gate_w, up_w, down_w = gate_w[0, 0], up_w[0, 0], down_w[0, 0]
    width, hidden = gate_w.shape
    products = 2 * 640 * width * hidden
    at = lax.axis_index("expert")
    sign = 1 - 2 * (lax.axis_index("section") % 2)
    where = jnp.stack([at // 2, at % 2, sign]).astype(jnp.int32)
    cotangent, fwd_acts = cotangent[0], fwd_acts[0]
    tabled = columns(routes_f[0], slots_f[0], gates_f[0], routes_b[0], slots_b[0], gates_b[0])
    x0 = jnp.concatenate([saved_acts[0], tabled], axis=-1)

    gr1, gl1 = hop(cotangent, 1, 0, 1), hop(cotangent, -1, 0, 1)
    xr1, xl1 = hop(x0, 1, 0), hop(x0, -1, 0)
    grad_out = hop(cotangent, 0, 0, 1)
    br1 = jnp.concatenate([xr1, gr1], axis=-1)
    bl1 = jnp.concatenate([xl1, gl1], axis=-1)
    br2, bl2 = hop(br1, 1, 0), hop(bl1, -1, 0)
    bu1, bv1, t0, t1r, t1l = both(both_near_kernel, where, (x0, grad_out, br1, bl1), (120, 120), 3, width, "b_near")
    bx1 = hop(bv1, 0, 1)
    layer_in = hop(after(fwd_acts, bv1), 0, 0, -1)
    br3 = hop(br2, 1, 0)
    br2, bl2 = after((br2, bl2), bv1)
    bu2, bv2, bend, t2r, t2l = both(both_mid_kernel, where, (br2, bl2), (80, 80, 80), 2, width, "b_mid")
    bl3, bx2 = hop(bend, -1, 0), hop(after(bv2, bx1), 0, 1)
    acts = after(fwd_acts, bend)
    fr1, fl1 = hop(acts, 1, 0, -1), hop(acts, -1, 0, -1)
    bu3, bv3, bs, bd, t3r = both(both_far_kernel, where, (br3, bl3), (CAP, 80, CAP, CAP), 1, width, "b_far")
    bx3 = hop(after(bv3, bx2), 0, 1)
    bs, bd = after((bs, bd), fr1, fl1)
    br4s, br4d = hop(bs, 1, 0), hop(bd, 1, 1)
    fr1, fl1 = after((fr1, fl1), bs)
    fr2, fl2 = hop(fr1, 1, 0), hop(fl1, -1, 0)
    fu1, fv1 = single(near_kernel, where, (layer_in, fr1, fl1, t0, t1r, t1l), (120, 120), width, "f_near")
    fx1 = hop(after(fv1, bx3), 0, 1)
    bu1 = after(bu1, fv1)
    *dx_rows, xb, gb, hb, da, db = call(
        functools.partial(backward_kernel, width),
        parts(width) + [shape(640, width)] * 2 + [shape(640, hidden)] * 3,
        (where, bu1, bu2, bx1, bx2, bu3, bl3, bx3, br4s, br4d, gate_w, up_w, down_w),
        5 * products,
        48,
        "backward",
        [pltpu.VMEM((640, width), F32)],
    )
    dy12, dw12, dy3, dl3, dw3, dr4s, dr4d = dx_rows
    dx3, dr4s, dr4d = hop(after(dw3, fx1), 0, 1), hop(dr4s, -1, 0), hop(dr4d, -1, 1)
    fr2, fl2 = after((fr2, fl2), dr4s, dr4d)
    fr3 = hop(fr2, 1, 0)
    fu2, fv2, fend = single(mid_kernel, where, (fr2, fl2, t2r, t2l), (80, 80, 80), width, "f_mid")
    fl3 = hop(fend, -1, 0)
    fx2 = hop(after(fv2, dx3), 0, 1)
    dright, dleft = summed(sum3_kernel, where, (dy3, dx3, dr4s, dr4d, dl3, t3r), 4, False, (128, 80), "dx_3")
    fr3, fl3 = after((fr3, fl3), dright)
    fu3, fv3, fs, fd = single(far_kernel, where, (fr3, fl3, t3r), (CAP, 80, CAP, CAP), width, "f_far")
    fr4s, fr4d, fx3 = hop(fs, 1, 0), hop(fd, 1, 1), hop(after(fv3, fx2), 0, 1)
    dright, dleft, dx12 = hop(dright, -1, 0), hop(dleft, 1, 0), hop(dw12, 0, 1)
    dright, dleft = summed(sum2_kernel, where, (dy12, dx12, dright, dleft, t2r, t2l), 4, False, (128, 128), "dx_2")
    dright, dleft = hop(dright, -1, 0), hop(dleft, 1, 0)
    yy12, yw12, yy3, yl3, yw3, yr4s, yr4d = call(
        forward_kernel,
        parts(width),
        (where, fu1, fu2, fx1, fx2, fu3, fl3, fx3, fr4s, fr4d, gate_w, up_w, down_w),
        3 * products,
        40,
        "forward",
        [pltpu.VMEM((640, width), BF16), pltpu.VMEM((640, width), F32)],
    )
    yr4s, yr4d, yx3 = hop(yr4s, -1, 0), hop(yr4d, -1, 1), hop(yw3, 0, 1)
    dright, dleft = summed(sum1_kernel, where, (dy12, dx12, dright, dleft, t1r, t1l), 4, False, (128, 128), "dx_1")
    dright, dleft = hop(dright, -1, 0), hop(dleft, 1, 0)
    yright, yleft = summed(sum3_kernel, where, (yy3, yx3, yr4s, yr4d, yl3, t3r), 0, True, (128, 80), "y_3")
    yright, yleft, yx12 = hop(yright, -1, 0), hop(yleft, 1, 0), hop(yw12, 0, 1)
    (input_grad,) = summed(sum0_kernel, where, (dy12, dx12, dright, dleft, grad_out, t0), 4, False, (128,), "dx_0")
    yright, yleft = summed(sum2_kernel, where, (yy12, yx12, yright, yleft, t2r, t2l), 0, True, (128, 128), "y_2")
    yright, yleft = hop(yright, -1, 0), hop(yleft, 1, 0)
    yright, yleft = summed(sum1_kernel, where, (yy12, yx12, yright, yleft, t1r, t1l), 0, True, (128, 128), "y_1")
    yright, yleft = hop(yright, -1, 0), hop(yleft, 1, 0)
    (fwd_out,) = summed(sum0_kernel, where, (yy12, yx12, yright, yleft, layer_in, t0), 0, True, (128,), "y_0")
    gate_grad = lax.dot_general(xb, da, TN, preferred_element_type=F32).astype(BF16)
    up_grad = lax.dot_general(xb, db, TN, preferred_element_type=F32).astype(BF16)
    down_grad = lax.dot_general(hb, gb, TN, preferred_element_type=F32).astype(BF16)
    return fwd_out[None], input_grad[None], gate_grad[None, None], up_grad[None, None], down_grad[None, None]


def solution(mesh):
    tokens = P("section", "expert", None)
    weights = P("section", "expert", None, None)
    return jax.shard_map(
        local,
        mesh=mesh,
        in_specs=(tokens,) * 3 + (weights,) * 3 + (tokens,) * 6,
        out_specs=(tokens,) * 2 + (weights,) * 3,
        check_vma=False,
    )
```

```python
import functools

import jax
import jax.numpy as jnp
from jax import lax
from jax.experimental import pallas as pl
from jax.experimental.pallas import tpu as pltpu
from jax.sharding import PartitionSpec as P

CAP = 40
NZ = 8
CODE = 64
F32 = jnp.float32
BF16 = jnp.bfloat16
AXES = ("section", "expert")
VMEM = pl.BlockSpec(memory_space=pltpu.VMEM)
SMEM = pl.BlockSpec(memory_space=pltpu.SMEM)


def hop(block, dz, flip, from_section=0):
    sections, experts = lax.axis_size("section"), lax.axis_size("expert")
    pairs = []
    for section in range(sections):
        sign = 1 - 2 * (section % 2)
        sender = (section + from_section) % sections
        for expert in range(experts):
            z, line = divmod(expert, 2)
            to = ((z + sign * dz) % NZ) * 2 + (line ^ flip)
            pairs.append((sender * experts + expert, section * experts + to))
    return lax.ppermute(block, AXES, pairs)


def after(value, *earlier):
    return lax.optimization_barrier((value, *earlier))[0]


def call(kernel, outs, args, flops, limit, name, scratch=()):
    size = sum(a.size * a.dtype.itemsize for a in args) + sum(
        o.size * jnp.dtype(o.dtype).itemsize for o in outs
    )
    return pl.pallas_call(
        kernel,
        out_shape=outs,
        in_specs=[SMEM] + [VMEM] * (len(args) - 1),
        out_specs=[VMEM] * len(outs),
        scratch_shapes=scratch,
        compiler_params=pltpu.CompilerParams(vmem_limit_bytes=limit << 20),
        cost_estimate=pl.CostEstimate(flops=flops, bytes_accessed=size, transcendentals=0),
        name=name,
    )(*args)


def shape(rows, width, dtype=BF16):
    return jax.ShapeDtypeStruct((rows, width), dtype)


def columns(routes_f, slots_f, gates_f, routes_b, slots_b, gates_b):
    gates = jnp.concatenate([gates_f, gates_b], axis=-1)
    high = lax.reduce_precision(gates, 8, 7)
    mid = lax.reduce_precision(gates - high, 8, 7)
    ints = [part.astype(F32) for part in (routes_f, routes_b, slots_f, slots_b)]
    every = jnp.concatenate([*ints, high, mid, gates - high - mid], axis=-1)
    return jnp.pad(every, ((0, 0), (0, 128 - every.shape[-1]))).astype(BF16)


def table_of(block, width):
    flat = block[:, width : width + 128].astype(F32).T
    codes = flat[0:8] * CODE + flat[8:16]
    return jnp.concatenate([codes, flat[16:24] + flat[24:32] + flat[32:40]], axis=0)


def group(where, at):
    return lax.shift_right_logical((where[0] + at * where[2]) & (NZ - 1), 1)


def onehot(where, table, first, at, flip):
    z = (where[0] + at * where[2]) & (NZ - 1)
    expert = z * 2 + (1 - where[1] if flip else where[1])
    code = table[pl.ds(first + group(where, at), 1), :]
    slot = lax.broadcasted_iota(jnp.int32, (CAP, code.shape[-1]), 0) + expert * CODE
    return (code == slot.astype(F32)).astype(F32)


def gate_row(where, table, first, at):
    return table[pl.ds(8 + first + group(where, at), 1), :]


def stack(*parts):
    return jnp.concatenate(parts, axis=0).astype(BF16)


def pick(where, table, first, block, places, gated):
    chosen = [onehot(where, table, first, at, flip) for at, flip in places]
    rows = jnp.dot(stack(*chosen), block, preferred_element_type=F32)
    if gated:
        gates = [
            jnp.sum(mask * gate_row(where, table, first, at), axis=1, keepdims=True)
            for mask, (at, _) in zip(chosen, places)
        ]
        rows = rows * jnp.concatenate(gates, axis=0)
    return [rows[i * CAP : (i + 1) * CAP] for i in range(len(places))]


HERE = ((0, 0), (0, 1))


def near_kernel(first, width, where, near, r1, l1, table0, table_r, table_l, own, other):
    got = [
        pick(where, table, first, block[...], HERE, False)
        for block, table in ((near, table0), (r1, table_r), (l1, table_l))
    ]
    own[...] = stack(*[g[0] for g in got])
    other[...] = stack(*[g[1] for g in got])


def mid_kernel(first, width, where, r2, l2, table_r, table_l, own, other, end):
    a = pick(where, table_r, first, r2[...], HERE, False)
    b = pick(where, table_l, first, l2[...], HERE + ((-1, 0), (-1, 1)), False)
    own[...] = stack(a[0], b[0])
    other[...] = stack(a[1], b[1])
    end[...] = stack(b[2], b[3])


def far_kernel(first, width, where, r3, l3, table3, own, other, same, cross):
    got = pick(where, table3, first, r3[...], HERE + ((1, 0), (1, 1)), False)
    own[...] = got[0].astype(BF16)
    other[...] = stack(got[1], l3[...].astype(F32)[CAP:])
    same[...] = got[2].astype(BF16)
    cross[...] = got[3].astype(BF16)


TABLE = (16, 128)


def halves(width):
    return (
        (False, slice(0, width), slice(0, width)),
        (True, slice(width + 128, 2 * width + 128), slice(width, 2 * width)),
    )


def both_near_kernel(width, where, near_x, near_g, r1, l1, own, other, *tables):
    for block, table in zip((near_x, r1, l1), tables):
        table[...] = table_of(block, width)
    for gated, of, cols in halves(width):
        near = near_g[...] if gated else near_x[:, cols]
        got = [
            pick(where, table, 4, block, HERE, gated)
            for block, table in zip((near, r1[:, of], l1[:, of]), tables)
        ]
        own[:, cols] = stack(*[g[0] for g in got])
        other[:, cols] = stack(*[g[1] for g in got])


def both_mid_kernel(width, where, r2, l2, own, other, end, table_r, table_l):
    table_r[...] = table_of(r2, width)
    table_l[...] = table_of(l2, width)
    for gated, of, cols in halves(width):
        a = pick(where, table_r, 4, r2[:, of], HERE, gated)
        b = pick(where, table_l, 4, l2[:, of], HERE + ((-1, 0), (-1, 1)), gated)
        own[:, cols] = stack(a[0], b[0])
        other[:, cols] = stack(a[1], b[1])
        end[:, cols] = stack(b[2], b[3])


def both_far_kernel(width, where, r3, l3, own, other, same, cross, table):
    table[...] = table_of(r3, width)
    for gated, of, cols in halves(width):
        got = pick(where, table, 4, r3[:, of], HERE + ((1, 0), (1, 1)), gated)
        own[:, cols] = got[0].astype(BF16)
        other[:, cols] = stack(got[1], l3[:, cols].astype(F32)[CAP:])
        same[:, cols] = got[2].astype(BF16)
        cross[:, cols] = got[3].astype(BF16)


def single(kernel, where, blocks, rows, width, name):
    return call(
        functools.partial(kernel, 0, width),
        [shape(r, width) for r in rows],
        (where, *blocks),
        2 * 240 * 128 * width,
        24,
        name,
    )


def both(kernel, where, blocks, rows, tables, width, name):
    outs = [shape(r, 2 * width) for r in rows] + [shape(*TABLE, F32)] * tables
    return call(functools.partial(kernel, width), outs, (where, *blocks), 4 * 240 * 128 * width, 32, name)


def assemble(near, far_units, x_ref, cols=slice(None)):
    x_ref[0:400, :] = stack(*[unit[:, cols].astype(F32) for unit in near])
    u3, l3, x3, r4s, r4d = far_units
    x_ref[400:480, :] = stack(u3[:, cols].astype(F32), l3[:, cols].astype(F32)[:CAP])
    x_ref[480:560, :] = x3[:, cols]
    x_ref[560:640, :] = stack(r4s[:, cols].astype(F32), r4d[:, cols].astype(F32))


PARTS = ((0, 200), (200, 400), (400, 440), (440, 480), (480, 560), (560, 600), (600, 640))


def part(o_ref, outs):
    for out, (first, last) in zip(outs, PARTS):
        out[...] = o_ref[first:last, :].astype(BF16)


def parts(width):
    return [shape(last - first, width) for first, last in PARTS]


TILE = 640
NT = (((1,), (1,)), ((), ()))
TN = (((0,), (0,)), ((), ()))


def tiles(body):
    @pl.loop(0, 640 // TILE)
    def _(i):
        body(pl.ds(pl.multiple_of(i * TILE, TILE), TILE))


def forward_kernel(where, *refs):
    units, (gate_w, up_w, down_w), outs, (x_ref, o_ref) = refs[:9], refs[9:12], refs[12:19], refs[19:]
    assemble(units[:4], units[4:], x_ref)

    @tiles
    def _(rows):
        x = x_ref[rows, :]
        a = jnp.dot(x, gate_w[...], preferred_element_type=F32)
        b = jnp.dot(x, up_w[...], preferred_element_type=F32)
        h = (a * jax.nn.sigmoid(a) * b).astype(BF16)
        o_ref[rows, :] = jnp.dot(h, down_w[...], preferred_element_type=F32)

    part(o_ref, outs)


def backward_kernel(width, where, *refs):
    units, (gate_w, up_w, down_w) = refs[:9], refs[9:12]
    outs, (x_ref, g_ref, h_ref, da_ref, db_ref), (o_ref,) = refs[12:19], refs[19:24], refs[24:]
    assemble(units[:4], units[4:], x_ref, slice(0, width))
    assemble(units[:4], units[4:], g_ref, slice(width, 2 * width))

    @tiles
    def _(rows):
        x = x_ref[rows, :]
        a = jnp.dot(x, gate_w[...], preferred_element_type=F32)
        b = jnp.dot(x, up_w[...], preferred_element_type=F32)
        sig = jax.nn.sigmoid(a)
        silu = a * sig
        h_ref[rows, :] = (silu * b).astype(BF16)
        dh = lax.dot_general(g_ref[rows, :], down_w[...], NT, preferred_element_type=F32)
        da = (dh * b * sig * (1.0 + a * (1.0 - sig))).astype(BF16)
        db = (dh * silu).astype(BF16)
        da_ref[rows, :] = da
        db_ref[rows, :] = db
        o_ref[rows, :] = lax.dot_general(da, gate_w[...], NT, preferred_element_type=F32) + lax.dot_general(
            db, up_w[...], NT, preferred_element_type=F32
        )

    part(o_ref, outs)


def placed(rows, masks):
    out, at = [], 0
    for start, mask in masks:
        if start > at:
            out.append(jnp.zeros((start - at, mask.shape[1]), F32))
        out.append(mask)
        at = start + CAP
    if at < rows:
        out.append(jnp.zeros((rows - at, masks[0][1].shape[1]), F32))
    return stack(*out)


def product(mask, rows):
    return lax.dot_general(mask, rows, TN, preferred_element_type=F32)


def weigh(where, table, first, at, gated, rows):
    if not gated:
        return rows
    row = gate_row(where, table, first, at)
    count = row.shape[-1]
    same = lax.broadcasted_iota(jnp.int32, (count, count), 0) == lax.broadcasted_iota(jnp.int32, (count, count), 1)
    return rows * jnp.sum(jnp.where(same, row, 0.0), axis=1, keepdims=True)


def local_sum(where, table, first, gated, own, other, start):
    total = 0.0
    for flip, ref in ((0, own), (1, other)):
        mask = placed(ref.shape[0], [(start, onehot(where, table, first, 0, flip))])
        total = total + product(mask, ref[...])
    return weigh(where, table, first, 0, gated, total)


def sum3_kernel(first, gated, where, y3, x3, r4s, r4d, l3, table, right, left):
    total = local_sum(where, table, first, gated, y3, x3, 0)
    ahead = 0.0
    for flip, ref in ((0, r4s), (1, r4d)):
        ahead = ahead + product(onehot(where, table, first, 1, flip).astype(BF16), ref[...])
    right[...] = (total + weigh(where, table, first, 1, gated, ahead)).astype(BF16)
    left[...] = stack(l3[...].astype(F32), x3[...].astype(F32)[CAP:])


def sum2_kernel(first, gated, where, y12, x12, got_r, got_l, table_r, table_l, right, left):
    right[...] = (got_r[...].astype(F32) + local_sum(where, table_r, first, gated, y12, x12, 120)).astype(BF16)
    masks = [(0, onehot(where, table_l, first, -1, 0)), (CAP, onehot(where, table_l, first, -1, 1))]
    ahead = weigh(where, table_l, first, -1, gated, product(placed(80, masks), got_l[...]))
    left[...] = (ahead + local_sum(where, table_l, first, gated, y12, x12, 160)).astype(BF16)


def sum1_kernel(first, gated, where, y12, x12, got_r, got_l, table_r, table_l, right, left):
    right[...] = (got_r[...].astype(F32) + local_sum(where, table_r, first, gated, y12, x12, 40)).astype(BF16)
    left[...] = (got_l[...].astype(F32) + local_sum(where, table_l, first, gated, y12, x12, 80)).astype(BF16)


def sum0_kernel(first, gated, where, y12, x12, got_r, got_l, base, table, out):
    total = local_sum(where, table, first, gated, y12, x12, 0)
    total = total + got_r[...].astype(F32) + got_l[...].astype(F32)
    out[...] = (base[...].astype(F32) + total).astype(BF16)


def summed(kernel, where, args, first, gated, rows, name):
    width = args[0].shape[-1]
    return call(
        functools.partial(kernel, first, gated),
        [shape(r, width) for r in rows],
        (where, *args),
        2 * 320 * 128 * width,
        24,
        name,
    )


def local(
    fwd_acts, saved_acts, cotangent, gate_w, up_w, down_w, routes_f, slots_f, gates_f, routes_b, slots_b, gates_b
):
    gate_w, up_w, down_w = gate_w[0, 0], up_w[0, 0], down_w[0, 0]
    width, hidden = gate_w.shape
    products = 2 * 640 * width * hidden
    at = lax.axis_index("expert")
    sign = 1 - 2 * (lax.axis_index("section") % 2)
    where = jnp.stack([at // 2, at % 2, sign]).astype(jnp.int32)
    cotangent, fwd_acts = cotangent[0], fwd_acts[0]
    tabled = columns(routes_f[0], slots_f[0], gates_f[0], routes_b[0], slots_b[0], gates_b[0])
    x0 = jnp.concatenate([saved_acts[0], tabled], axis=-1)

    gr1, gl1 = hop(cotangent, 1, 0, 1), hop(cotangent, -1, 0, 1)
    xr1, xl1 = hop(x0, 1, 0), hop(x0, -1, 0)
    grad_out = hop(cotangent, 0, 0, 1)
    br1 = jnp.concatenate([xr1, gr1], axis=-1)
    bl1 = jnp.concatenate([xl1, gl1], axis=-1)
    br2, bl2 = hop(br1, 1, 0), hop(bl1, -1, 0)
    bu1, bv1, t0, t1r, t1l = both(both_near_kernel, where, (x0, grad_out, br1, bl1), (120, 120), 3, width, "b_near")
    bx1 = hop(bv1, 0, 1)
    layer_in = hop(after(fwd_acts, bv1), 0, 0, -1)
    br3 = hop(br2, 1, 0)
    br2, bl2 = after((br2, bl2), bv1)
    bu2, bv2, bend, t2r, t2l = both(both_mid_kernel, where, (br2, bl2), (80, 80, 80), 2, width, "b_mid")
    bl3, bx2 = hop(bend, -1, 0), hop(after(bv2, bx1), 0, 1)
    acts = after(fwd_acts, bend)
    fr1, fl1 = hop(acts, 1, 0, -1), hop(acts, -1, 0, -1)
    bu3, bv3, bs, bd, t3r = both(both_far_kernel, where, (br3, bl3), (CAP, 80, CAP, CAP), 1, width, "b_far")
    bx3 = hop(after(bv3, bx2), 0, 1)
    bs, bd = after((bs, bd), fr1, fl1)
    br4s, br4d = hop(bs, 1, 0), hop(bd, 1, 1)
    fr1, fl1 = after((fr1, fl1), bs)
    fr2, fl2 = hop(fr1, 1, 0), hop(fl1, -1, 0)
    fu1, fv1 = single(near_kernel, where, (layer_in, fr1, fl1, t0, t1r, t1l), (120, 120), width, "f_near")
    fx1 = hop(after(fv1, bx3), 0, 1)
    bu1 = after(bu1, fv1)
    *dx_rows, xb, gb, hb, da, db = call(
        functools.partial(backward_kernel, width),
        parts(width) + [shape(640, width)] * 2 + [shape(640, hidden)] * 3,
        (where, bu1, bu2, bx1, bx2, bu3, bl3, bx3, br4s, br4d, gate_w, up_w, down_w),
        5 * products,
        48,
        "backward",
        [pltpu.VMEM((640, width), F32)],
    )
    dy12, dw12, dy3, dl3, dw3, dr4s, dr4d = dx_rows
    dx3, dr4s, dr4d = hop(dw3, 0, 1), hop(dr4s, -1, 0), hop(dr4d, -1, 1)
    fr2, fl2 = after((fr2, fl2), dr4s, dr4d)
    fr3 = hop(fr2, 1, 0)
    fu2, fv2, fend = single(mid_kernel, where, (fr2, fl2, t2r, t2l), (80, 80, 80), width, "f_mid")
    fl3 = hop(fend, -1, 0)
    fx2 = hop(fv2, 0, 1)
    dright, dleft = summed(sum3_kernel, where, (dy3, dx3, dr4s, dr4d, dl3, t3r), 4, False, (128, 80), "dx_3")
    dright, dleft = hop(dright, -1, 0), hop(dleft, 1, 0)
    fr3, fl3 = after((fr3, fl3), dright, dleft)
    fu3, fv3, fs, fd = single(far_kernel, where, (fr3, fl3, t3r), (CAP, 80, CAP, CAP), width, "f_far")
    fr4s, fr4d, fx3 = hop(fs, 1, 0), hop(fd, 1, 1), hop(fv3, 0, 1)
    dx12 = hop(dw12, 0, 1)
    dright, dleft = summed(sum2_kernel, where, (dy12, dx12, dright, dleft, t2r, t2l), 4, False, (128, 128), "dx_2")
    dright, dleft = hop(dright, -1, 0), hop(dleft, 1, 0)
    yy12, yw12, yy3, yl3, yw3, yr4s, yr4d = call(
        forward_kernel,
        parts(width),
        (where, fu1, fu2, fx1, fx2, fu3, fl3, fx3, fr4s, fr4d, gate_w, up_w, down_w),
        3 * products,
        40,
        "forward",
        [pltpu.VMEM((640, width), BF16), pltpu.VMEM((640, width), F32)],
    )
    yr4s, yr4d, yx3 = hop(yr4s, -1, 0), hop(yr4d, -1, 1), hop(yw3, 0, 1)
    dright, dleft = summed(sum1_kernel, where, (dy12, dx12, dright, dleft, t1r, t1l), 4, False, (128, 128), "dx_1")
    dright, dleft = hop(dright, -1, 0), hop(dleft, 1, 0)
    yright, yleft = summed(sum3_kernel, where, (yy3, yx3, yr4s, yr4d, yl3, t3r), 0, True, (128, 80), "y_3")
    yright, yleft, yx12 = hop(yright, -1, 0), hop(yleft, 1, 0), hop(yw12, 0, 1)
    (input_grad,) = summed(sum0_kernel, where, (dy12, dx12, dright, dleft, grad_out, t0), 4, False, (128,), "dx_0")
    yright, yleft = summed(sum2_kernel, where, (yy12, yx12, yright, yleft, t2r, t2l), 0, True, (128, 128), "y_2")
    yright, yleft = hop(yright, -1, 0), hop(yleft, 1, 0)
    yright, yleft = summed(sum1_kernel, where, (yy12, yx12, yright, yleft, t1r, t1l), 0, True, (128, 128), "y_1")
    yright, yleft = hop(yright, -1, 0), hop(yleft, 1, 0)
    (fwd_out,) = summed(sum0_kernel, where, (yy12, yx12, yright, yleft, layer_in, t0), 0, True, (128,), "y_0")
    gate_grad = lax.dot_general(xb, da, TN, preferred_element_type=F32).astype(BF16)
    up_grad = lax.dot_general(xb, db, TN, preferred_element_type=F32).astype(BF16)
    down_grad = lax.dot_general(hb, gb, TN, preferred_element_type=F32).astype(BF16)
    return fwd_out[None], input_grad[None], gate_grad[None, None], up_grad[None, None], down_grad[None, None]


def solution(mesh):
    tokens = P("section", "expert", None)
    weights = P("section", "expert", None, None)
    return jax.shard_map(
        local,
        mesh=mesh,
        in_specs=(tokens,) * 3 + (weights,) * 3 + (tokens,) * 6,
        out_specs=(tokens,) * 2 + (weights,) * 3,
        check_vma=False,
    )
```
